32 devices in a mesh: lon: 8 (over z, y), lat: 4 (over x, core).
Axes of the slice: x: 2, y: 2, z: 4, core: 2. Of those that a mesh axis runs over, the one named last changes fastest.
Arguments:
- obs_values: bfloat16 [16384, 128], P(('lon', 'lat')), may hold values from -6 to 6
- obs_owner: int32 [16384, 1], P(('lon', 'lat')), may hold values from 0 to 7; in each aligned block of 512 rows (0 to 511, 512 to 1023, ...) at most 128 rows name the same one
- obs_cell: int32 [16384], P(('lon', 'lat')), may hold values from 0 to 2047
- obs_count: int32 [32], P(('lon', 'lat')), may hold values from 256 to 512, as said below
- obs_map: bfloat16 [128, 384], replicated, may hold values from -0.5 to 0.5
- column_mix: float32 [384, 384], replicated, may hold values from -0.3125 to 0.3125
- center: float32 [128, 512], P('lon', 'lat'), may hold values from 0.4 to 1
- neighbor: float32 [4, 128, 512], P(None, 'lon', 'lat'), may hold values from 0.08 to 0.3
Outputs:
- gradient: float32 [384, 128, 512], P(None, 'lon', 'lat')
The draws below stay inside these ranges and needn't reach their ends.
Inputs may be any that keep to these rules, and one draw needn't show every extreme that they name: `obs_owner`: among the rows of one device at most 128 name the same longitude block, and some block is named by exactly 128 of them. `obs_count`: rows of a device past its count are not live; some device has all 512 rows live.
All inputs are finite; a program needn't handle non-finite values.
Results may differ from the reference program's by a relative error of at most 0.0029.
Values may be sent and summed in bfloat16 or wider, within the bound.
A program may use at most 64 MiB of HBM per device.

```python
import math
import jax
import jax.numpy as jnp
import numpy as np
from jax import lax

VALS = 128
STEPS = 2
CLON = 16
CLAT = 128
OBS_DEV = 512
COLDEPTH = 384
LON_BLOCKS = 8
LAT_BLOCKS = 4
NBLOCKS = 32
CAP = 128
NLON = 128
NLAT = 512
OBS = 16384


def draw_obs_count(key, part):
    first_key, second_key = jax.random.split(jax.random.fold_in(key, 11))
    counted = jax.random.randint(first_key, (NBLOCKS,), OBS_DEV // 2, OBS_DEV + 1, dtype=jnp.int32)
    chosen = jax.random.randint(second_key, (), 0, NBLOCKS, dtype=jnp.int32)
    return counted.at[chosen].set(OBS_DEV)


def touch_ends(entries, key, smallest, top_value):
    longest = entries.shape.index(max(entries.shape))
    spots = []
    for shift in (0, 1):
        where = [jax.random.randint(jax.random.fold_in(key, axis), (), 0, length) for axis, length in enumerate(entries.shape)]
        where[longest] = (where[longest] + shift) % entries.shape[longest]
        spots.append(tuple(where))
    return entries.at[spots[0]].set(smallest).at[spots[1]].set(top_value)


def levels(own_key, shape, cuts, low, largest):
    factor_of, own = 1.0, jax.random.fold_in(own_key, 6)
    for axis_at, parts in cuts:
        steps = jnp.exp(jax.random.uniform(jax.random.fold_in(own, axis_at), (parts,), jnp.float32, low / len(cuts), largest / len(cuts)))
        factor_of = factor_of * jnp.repeat(steps, shape[axis_at] // parts).reshape([-1 if axis == axis_at else 1 for axis in range(len(shape))])
    return factor_of


def deal_out(own_key, own, number, rows, count, top, reach, slope):
    ranking = jax.random.permutation(own_key, count)
    heavy_load, usual = load_shares(count, rows * top, reach, slope, True), load_shares(count, rows * top, reach, slope, False)
    places = jnp.arange(count)

    def named(sizes, offset_by):
        used = int((sizes > 0).sum())
        fixed = max(1, used // 4)
        moved = fixed + (places - fixed + offset_by * (used - fixed)) % max(1, count - fixed)
        return jnp.zeros((count,), jnp.int32).at[ranking[jnp.where(places < fixed, places, moved)]].set(jnp.asarray(sizes, jnp.int32))

    sizes = jnp.where(number % 4 == 0, named(heavy_load, number // 4), named(usual, number - number // 4 - 1))
    mixed = jax.random.permutation(jax.random.fold_in(own, 3), count)
    donor, sink = mixed[0:count // 2 * 2:2], mixed[1:count // 2 * 2:2]
    room = jnp.minimum(sizes[donor] - 1, reach - sizes[sink]) // 2
    room = jnp.where((donor == ranking[0]) | (sink == ranking[0]) | (sizes[sink] == 0), 0, jnp.maximum(room, 0))
    moved = jax.random.randint(jax.random.fold_in(own, 4), (count // 2,), 0, 1 << 20) % (room + 1)
    sizes = sizes.at[donor].add(-moved).at[sink].add(moved)
    members = jnp.searchsorted(jnp.cumsum(sizes), jnp.arange(rows * top), side="right").astype(jnp.int32)
    listing = members.reshape(top, rows).T
    listing = listing[jax.random.permutation(jax.random.fold_in(own, 1), rows)]
    offset_by = jax.random.randint(jax.random.fold_in(own, 2), (rows, 1), 0, top)
    return jnp.take_along_axis(listing, (jnp.arange(top)[None, :] + offset_by) % top, axis=1)


def load_shares(number_of, total, most, lean, full):
    portions = [(1 << 20) // math.isqrt(rank ** lean) + 1 for rank in range(1, number_of + 1)]
    largest = most if full else min(most, max(-(-total // number_of), total * portions[0] // sum(portions)))
    least = 1 if total - largest >= number_of - 1 else 0
    counts, surplus = [largest] + [least] * (number_of - 1), total - largest - least * (number_of - 1)
    while surplus > 0:
        candidates = [i for i in range(1, number_of) if counts[i] < largest] or [i for i in range(1, number_of) if counts[i] < most]
        whole, budget = sum([portions[i] for i in candidates]), surplus
        for i in candidates:
            extra = min(most - counts[i], max(1, budget * portions[i] // whole), surplus)
            counts[i] = counts[i] + extra
            surplus = surplus - extra
    return np.array(counts)


def gaussian(own_key, dims, scale, limit, cuts=(), held_as=jnp.bfloat16):
    result = jax.random.normal(own_key, dims, jnp.float32) * scale
    if len(cuts) > 0:
        result = levels(own_key, dims, cuts, -0.22, 0.18) * result
    return jnp.clip(result, min=-limit, max=limit).astype(held_as)


def setup_inputs(seed: int = 0) -> dict:
    streams_of = jax.random.split(jax.random.key(seed), 9)
    obs_values = gaussian(streams_of[0], (OBS, VALS), 1.0, 6.0, ((0, 32),))
    obs_owner_keys = jax.random.split(jax.random.fold_in(streams_of[1], 1), OBS // OBS_DEV)
    obs_owner_turns = jax.random.permutation(jax.random.fold_in(streams_of[1], 3), OBS // OBS_DEV)
    obs_owner = jax.vmap(lambda own, number: deal_out(jax.random.fold_in(streams_of[1], 2), own, number, OBS_DEV, LON_BLOCKS, 1, CAP, 2))(obs_owner_keys, obs_owner_turns).reshape((OBS, 1))
    obs_cell = touch_ends(jax.random.randint(streams_of[2], (OBS,), 0, CLON * CLAT), jax.random.fold_in(streams_of[2], 1), 0, (CLON * CLAT) - 1).astype(jnp.int32)
    obs_count = draw_obs_count(jax.random.fold_in(streams_of[8], 71), 0)
    obs_map = gaussian(streams_of[4], (VALS, COLDEPTH), VALS ** -0.5, 0.5)
    column_mix = gaussian(streams_of[5], (COLDEPTH, COLDEPTH), COLDEPTH ** -0.5, 0.3125, (), jnp.float32)
    center = jnp.clip(0.4 + 0.6 * jax.random.uniform(streams_of[6], (NLON, NLAT), jnp.float32) ** levels(streams_of[6], (NLON, NLAT), ((0, 8), (1, 4)), -0.2, 0.2), 0.4, 1.0)
    neighbor = jnp.clip(jnp.exp(math.log(0.3) - 1.3217559 * jax.random.uniform(streams_of[7], (4, NLON, NLAT), jnp.float32) ** levels(streams_of[7], (4, NLON, NLAT), ((1, 8), (2, 4)), -0.2, 0.2)), 0.08, 0.3)
    return dict(obs_values=obs_values, obs_owner=obs_owner, obs_cell=obs_cell, obs_count=obs_count, obs_map=obs_map, column_mix=column_mix, center=center, neighbor=neighbor)


def reference(obs_values, obs_owner, obs_cell, obs_count, obs_map, column_mix, center, neighbor):
    extent = column_mix.shape[0]
    owner_list = obs_owner[:, 0]

    def add_block(block_id, totals):
        block_id = jnp.asarray(block_id, jnp.int32)
        first_row = block_id * OBS_DEV
        values = lax.dynamic_slice_in_dim(obs_values, first_row, OBS_DEV, 0)
        mapped = jnp.dot(values, obs_map, preferred_element_type=jnp.float32).astype(jnp.bfloat16)
        mapped = lax.optimization_barrier(mapped).astype(totals.dtype)
        owners = lax.dynamic_slice_in_dim(owner_list, first_row, OBS_DEV, 0)
        places = lax.dynamic_slice_in_dim(obs_cell, first_row, OBS_DEV, 0)
        lat_band = block_id % LAT_BLOCKS
        lon_index = owners * CLON + places // CLAT
        lat_index = lat_band * CLAT + places % CLAT
        flat_index = (lon_index * NLAT + lat_index).astype(jnp.int32)
        living = jnp.arange(OBS_DEV, dtype=jnp.int32) < obs_count[block_id]
        mapped = jnp.where(living[:, None], mapped, jnp.zeros_like(mapped))
        return totals.at[flat_index].add(mapped)

    totals = lax.fori_loop(0, NBLOCKS, add_block, jnp.zeros((NLON * NLAT, extent), jnp.float32))
    adjoint = totals.T.reshape(extent, NLON, NLAT)
    for section in range(STEPS):
        mixed = jnp.einsum("ab,acd->bcd", column_mix, adjoint, precision=lax.Precision.HIGHEST)
        from_west = jnp.roll(mixed, 1, axis=1)
        from_east = jnp.roll(mixed, -1, axis=1)
        padded = jnp.pad(mixed, ((0, 0), (0, 0), (1, 1)))
        from_south = padded[:, :, :-2]
        from_north = padded[:, :, 2:]
        adjoint = (center * mixed + neighbor[0] * from_west + neighbor[1] * from_east
                   + neighbor[2] * from_south + neighbor[3] * from_north)
    return adjoint
```

```python
import functools

import jax
import jax.numpy as jnp
from jax import lax
from jax.experimental import pallas as pl
from jax.experimental.pallas import tpu as pltpu
from jax.sharding import PartitionSpec as P

STEPS = 2
MESH = pl.DeviceIdType.MESH
HIGHEST = lax.Precision.HIGHEST
NT = (((1,), (1,)), ((), ()))
BF16 = jnp.bfloat16
F32 = jnp.float32


def with_halo(x, sides, width, wrap):
    for axis, dim in sides:
        size, length = (lax.axis_size(axis), x.shape[dim])
        up = [(i, (i + 1) % size) for i in range(size if wrap else size - 1)]
        down = [(j, i) for i, j in up]
        last = lax.slice_in_dim(x, length - width, length, axis=dim)
        first = lax.slice_in_dim(x, 0, width, axis=dim)
        before = lax.ppermute(last, axis, up)
        after = lax.ppermute(first, axis, down)
        x = jnp.concatenate([before, x, after], axis=dim)
    return x


def stencil(spread, middle, weights):
    return (
        middle * spread[:, 1:-1, 1:-1]
        + weights[0] * spread[:, :-2, 1:-1]
        + weights[1] * spread[:, 2:, 1:-1]
        + weights[2] * spread[:, 1:-1, :-2]
        + weights[3] * spread[:, 1:-1, 2:]
    )


def plain(obs_values, obs_owner, obs_cell, obs_count, obs_map, column_mix, center, neighbor):
    lon_count = lax.axis_size("lon")
    rows, width = obs_values.shape
    capacity = 2 * rows // lon_count
    slots = lon_count * capacity
    lon_cells, lat_cells = center.shape
    owners = obs_owner[:, 0]
    living = jnp.arange(rows, dtype=jnp.int32) < obs_count[0]
    number = jnp.arange(rows, dtype=jnp.int32)
    same = (owners[:, None] == owners[None, :]) & (number[None, :] < number[:, None])
    earlier = jnp.sum(same.astype(jnp.int32), axis=1)
    target = jnp.where(living, owners * capacity + earlier, -1)
    chosen = jnp.arange(slots, dtype=jnp.int32)[:, None] == target[None, :]
    packed = jnp.dot(chosen.astype(BF16), obs_values, preferred_element_type=F32).astype(BF16)
    places = jnp.sum(jnp.where(chosen, obs_cell[None, :] + 1, 0), axis=1) - 1
    packed = packed.reshape(lon_count, capacity, width)
    places = places.reshape(lon_count, capacity)
    packed = lax.all_to_all(packed, "lon", split_axis=0, concat_axis=0, tiled=True)
    places = lax.all_to_all(places, "lon", split_axis=0, concat_axis=0, tiled=True)
    cells = jnp.arange(lon_cells * lat_cells, dtype=jnp.int32)
    onehot = (places.reshape(slots)[:, None] == cells[None, :]).astype(BF16)
    adjoint = lax.dot_general(
        packed.reshape(slots, width), onehot, (((0,), (0,)), ((), ())), preferred_element_type=F32
    ).reshape(width, lon_cells, lat_cells)
    weight = obs_map.astype(F32)
    for section in range(STEPS):
        weight = jnp.dot(weight, column_mix, precision=HIGHEST)
        spread = with_halo(adjoint, (("lon", 1),), 1, True)
        spread = with_halo(spread, (("lat", 2),), 1, False)
        adjoint = stencil(spread, center, neighbor)
    return jnp.einsum("vb,vij->bij", weight, adjoint, precision=HIGHEST)


def iota(shape, dim):
    return lax.broadcasted_iota(jnp.int32, shape, dim)


def onehot_of(labels, count):
    return jnp.where(iota((count, labels.shape[1]), 0) == labels, 1.0, 0.0).astype(BF16)


def route_kernel(
    lon_n, lat_n,
    values, owner, cell, count, obs_map, mix, center, neighbor,
    f_out, halo_out, edge_out, corner_out, wlon_out, wlat_out, weight_out,
    send, recv, fsend, halo, esend, edge, corner, wlon_send, wlon, wlat_send, wlat,
    a_send, a_recv, h_send, h_recv,
):
    me, band = lax.axis_index("lon"), lax.axis_index("lat")
    east, west = lax.rem(me + 1, lon_n), lax.rem(me + lon_n - 1, lon_n)
    north, south = lax.rem(band + 1, lat_n), lax.rem(band + lat_n - 1, lat_n)
    barrier = pltpu.get_barrier_semaphore()
    partners = [(lax.rem(me + k, lon_n), band) for k in range(1, lon_n)]
    partners += [(a, b) for a in (me, east, west) for b in (north, south)]
    for partner in partners:
        pl.semaphore_signal(barrier, inc=1, device_id=partner, device_id_type=MESH)

    lon_cells, lat_cells = center.shape
    rows, width = values.shape
    cap = 2 * rows // lon_n
    own, place = owner[...], cell[...]
    owned = iota((16, rows), 0) == own
    before = jnp.where(iota((rows, rows), 0) < iota((rows, rows), 1), 1.0, 0.0).astype(BF16)
    prior = jnp.dot(jnp.where(owned, 1.0, 0.0).astype(BF16), before, preferred_element_type=F32)
    position = jnp.sum(jnp.where(owned, prior, 0.0), axis=0, keepdims=True).astype(jnp.int32)
    target = jnp.where(iota((1, rows), 1) < count[0], own * cap + position, -1)
    chosen = onehot_of(target, lon_n * cap)
    i, j = place // lat_cells, place % lat_cells
    side = jnp.where(j < 2, j, jnp.where(j >= lat_cells - 2, j - (lat_cells - 4), 4))
    sub = iota((16, rows), 0)
    labels = jnp.where(
        sub == 0,
        i // 2,
        jnp.where(sub == 1, (i % 2) * lat_cells + j, jnp.where(sub == 2, side * lon_cells + i, 0)),
    ).astype(F32)
    turned = jnp.concatenate([values[...].astype(F32).T, labels], axis=0).astype(BF16)
    packed = lax.dot_general(turned, chosen, NT, preferred_element_type=F32).astype(BF16)
    for o in range(lon_n):
        send[o] = packed[:, o * cap : (o + 1) * cap]

    weights = [center[...]] + [neighbor[k] for k in range(4)]
    wlon_send[...] = jnp.zeros_like(wlon_send)
    for k in range(5):
        wlon_send[0, k : k + 1, :] = weights[k][0:1]
        wlon_send[1, k : k + 1, :] = weights[k][lon_cells - 1 : lon_cells]
    stacked = jnp.concatenate(weights + [jnp.zeros((128 - 5 * lon_cells, lat_cells), F32)], axis=0).T
    wlat_send[0] = stacked[0:8]
    wlat_send[1] = stacked[lat_cells - 8 : lat_cells]

    pl.semaphore_wait(barrier, len(partners))

    def copy(src, dst, sem_out, sem_in, device):
        return pltpu.make_async_remote_copy(
            src_ref=src, dst_ref=dst, send_sem=sem_out, recv_sem=sem_in,
            device_id=device, device_id_type=MESH,
        )

    moves = []
    for k in range(1, lon_n):
        to = lax.rem(me + k, lon_n)
        moves.append(copy(send.at[to], recv.at[k], a_send.at[k - 1], a_recv.at[k - 1], (to, band)))
        moves[-1].start()
    later = []

    def start_later(src, dst, device):
        n = len(later)
        later.append(copy(src, dst, h_send.at[n], h_recv.at[n], device))
        later[-1].start()

    start_later(wlon_send.at[1], wlon.at[0], (east, band))
    start_later(wlon_send.at[0], wlon.at[1], (west, band))
    start_later(wlat_send.at[1], wlat.at[0], (me, north))
    start_later(wlat_send.at[0], wlat.at[1], (me, south))
    recv[0] = send[me]

    weight = obs_map[...].astype(F32)
    for section in range(STEPS):
        weight = jnp.dot(weight, mix[...], precision=HIGHEST, preferred_element_type=F32)
    weight = weight.T
    high = weight.astype(BF16)
    low = (weight - high.astype(F32)).astype(BF16)
    weight_out[...] = jnp.concatenate([high, high, low], axis=1)

    for move in moves:
        move.wait()

    arrived = jnp.concatenate([recv[k, 0:width, :] for k in range(lon_n)], axis=1)
    marks = jnp.concatenate([recv[k, width : width + 16, :] for k in range(lon_n)], axis=1)
    marks = marks.astype(F32).astype(jnp.int32)
    pair, column, rim = marks[0:1], marks[1:2], marks[2:3]
    columns = onehot_of(column, 2 * lat_cells)

    def masked(p):
        return arrived * jnp.where(pair == p, 1.0, 0.0).astype(BF16)

    def spread(pairs):
        left = jnp.concatenate([masked(p) for p in pairs], axis=0)
        out = lax.dot_general(left, columns, NT, preferred_element_type=F32).astype(BF16)
        for n, p in enumerate(pairs):
            for half in range(2):
                yield 2 * p + half, out[n * width : (n + 1) * width, half * lat_cells : (half + 1) * lat_cells]

    pairs = lon_cells // 2
    for n, (at, block) in enumerate(spread((0, pairs - 1))):
        fsend[n] = block
        f_out[at] = block
    start_later(fsend.at[pl.ds(2, 2)], halo.at[pl.ds(0, 2)], (east, band))
    start_later(fsend.at[pl.ds(0, 2)], halo.at[pl.ds(2, 2)], (west, band))
    rims = onehot_of(rim, 4 * lon_cells)
    esend[...] = lax.dot_general(rims, arrived, NT, preferred_element_type=F32).astype(BF16)
    start_later(esend.at[pl.ds(32, 32)], edge.at[pl.ds(0, 32)], (me, north))
    start_later(esend.at[pl.ds(0, 32)], edge.at[pl.ds(32, 32)], (me, south))
    start_later(esend.at[pl.ds(48, 16)], corner.at[0], (east, north))
    start_later(esend.at[pl.ds(0, 16)], corner.at[1], (east, south))
    start_later(esend.at[pl.ds(48, 16)], corner.at[2], (west, north))
    start_later(esend.at[pl.ds(0, 16)], corner.at[3], (west, south))
    for at, block in spread(range(1, pairs - 1)):
        f_out[at] = block
    for move in later:
        move.wait()
    halo_out[...] = halo[...]
    edge_out[0:64] = edge[...]
    edge_out[64:80] = esend[0:16]
    edge_out[80:96] = esend[48:64]
    corner_out[...] = corner[...]
    wlon_out[...] = wlon[...]
    wlat_out[...] = wlat[...]


def apply_kernel(
    lat_n, f, halo, edge, corner, wlon, wlat, weight, center, neighbor, out, first, grid_values
):
    lon_cells, lat_cells = center.shape
    width = f.shape[1]

    @pl.when(pl.program_id(0) == 0)
    def _():
        band = lax.axis_index("lat")
        keeps = [jnp.where(band > 0, 1.0, 0.0), jnp.where(band < lat_n - 1, 1.0, 0.0)]
        rim = edge[...].astype(F32)
        south2, south1, north1, north2, inner_s, inner_n = (rim[16 * n : 16 * (n + 1)] for n in range(6))
        corners = corner[...].astype(F32)
        cws, cwn, ces, cen = corners[0, 15:16], corners[1, 15:16], corners[2, 0:1], corners[3, 0:1]

        def rim_step(turned, here, west, east, below, above):
            w = [turned[16 * k : 16 * (k + 1)] for k in range(5)]
            up = jnp.concatenate([west, here[:-1]], axis=0)
            down = jnp.concatenate([here[1:], east], axis=0)
            return w[0] * here + w[1] * up + w[2] * down + w[3] * below + w[4] * above

        tall = jnp.zeros((120, 128), F32)
        ws = jnp.concatenate([wlat[0], tall], axis=0).T[:, 7:8]
        wn = jnp.concatenate([wlat[1], tall], axis=0).T[:, 0:1]
        step_s = rim_step(ws, south1, cws, ces, south2, inner_s)
        step_n = rim_step(wn, north1, cwn, cen, inner_n, north2)
        table = jnp.concatenate(
            [south1 * keeps[0], north1 * keeps[1], step_s * keeps[0], step_n * keeps[1],
             cws * keeps[0], cwn * keeps[1], ces * keeps[0], cen * keeps[1],
             jnp.zeros((60, width), F32)], axis=0,
        ).T
        lane = iota((width, lat_cells), 1)

        def value(n):
            if n < 0:
                return halo[n + 2].astype(F32)
            return halo[n - lon_cells + 2].astype(F32) if n >= lon_cells else f[n].astype(F32)

        def weights_at(n):
            if n < 0:
                return [wlon[0, k : k + 1, :] for k in range(5)]
            if n >= lon_cells:
                return [wlon[1, k : k + 1, :] for k in range(5)]
            return [center[n : n + 1, :]] + [neighbor[k, n : n + 1, :] for k in range(4)]

        def step(n, here, west, east, s, t):
            w = weights_at(n)
            below = jnp.where(lane == 0, table[:, s : s + 1], pltpu.roll(here, 1, 1))
            above = jnp.where(lane == lat_cells - 1, table[:, t : t + 1], pltpu.roll(here, lat_cells - 1, 1))
            return w[0] * here + w[1] * west + w[2] * east + w[3] * below + w[4] * above

        for n in range(-1, lon_cells + 1):
            s, t = (64, 65) if n < 0 else (66, 67) if n >= lon_cells else (n, 16 + n)
            first[n + 1] = step(n, value(n), value(n - 1), value(n + 1), s, t)
        for n in range(lon_cells):
            done = step(n, first[n + 1], first[n], first[n + 2], 32 + n, 48 + n)
            high = done.astype(BF16)
            at = slice(n * lat_cells, (n + 1) * lat_cells)
            grid_values[0:width, at] = high
            grid_values[width : 2 * width, at] = (done - high.astype(F32)).astype(BF16)
            grid_values[2 * width : 3 * width, at] = high

    result = jnp.dot(weight[...], grid_values[...], preferred_element_type=F32)
    chunk = weight.shape[0]
    for n in range(lon_cells):
        out[pl.ds(n, chunk, stride=lon_cells), :] = result[:, n * lat_cells : (n + 1) * lat_cells]


def fast(obs_values, obs_owner, obs_cell, obs_count, obs_map, column_mix, center, neighbor):
    lon_n, lat_n = lax.axis_size("lon"), lax.axis_size("lat")
    rows, width = obs_values.shape
    extent = column_mix.shape[0]
    lon_cells, lat_cells = center.shape
    cap = 2 * rows // lon_n
    vmem, shape = pl.BlockSpec(memory_space=pltpu.VMEM), jax.ShapeDtypeStruct
    parts = pl.pallas_call(
        functools.partial(route_kernel, lon_n, lat_n),
        out_shape=[
            shape((lon_cells, width, lat_cells), BF16),
            shape((4, width, lat_cells), BF16),
            shape((96, width), BF16),
            shape((4, 16, width), BF16),
            shape((2, 8, lat_cells), F32),
            shape((2, 8, 128), F32),
            shape((extent, 3 * width), BF16),
        ],
        in_specs=[vmem] * 3 + [pl.BlockSpec(memory_space=pltpu.SMEM)] + [vmem] * 4,
        out_specs=[vmem] * 7,
        scratch_shapes=[
            pltpu.VMEM((lon_n, width + 16, cap), BF16),
            pltpu.VMEM((lon_n, width + 16, cap), BF16),
            pltpu.VMEM((4, width, lat_cells), BF16),
            pltpu.VMEM((4, width, lat_cells), BF16),
            pltpu.VMEM((64, width), BF16),
            pltpu.VMEM((64, width), BF16),
            pltpu.VMEM((4, 16, width), BF16),
            pltpu.VMEM((2, 8, lat_cells), F32),
            pltpu.VMEM((2, 8, lat_cells), F32),
            pltpu.VMEM((2, 8, 128), F32),
            pltpu.VMEM((2, 8, 128), F32),
            pltpu.SemaphoreType.DMA((lon_n - 1,)),
            pltpu.SemaphoreType.DMA((lon_n - 1,)),
            pltpu.SemaphoreType.DMA((12,)),
            pltpu.SemaphoreType.DMA((12,)),
        ],
        compiler_params=pltpu.CompilerParams(
            collective_id=0, has_side_effects=True, vmem_limit_bytes=40 * 2**20
        ),
    )(obs_values, obs_owner.reshape(1, rows), obs_cell.reshape(1, rows), obs_count, obs_map, column_mix, center, neighbor)
    f, halo, edge, corner, wlon, wlat, weight = parts
    chunk = extent // 6
    whole = [
        pl.BlockSpec(x.shape, functools.partial(lambda d, n: (0,) * d, x.ndim))
        for x in (f, halo, edge, corner, wlon, wlat)
    ]
    out = pl.pallas_call(
        functools.partial(apply_kernel, lat_n),
        grid=(extent // chunk,),
        out_shape=shape((extent * lon_cells, lat_cells), F32),
        in_specs=whole + [
            pl.BlockSpec((chunk, 3 * width), lambda n: (n, 0)),
            pl.BlockSpec(center.shape, lambda n: (0, 0)),
            pl.BlockSpec(neighbor.shape, lambda n: (0, 0, 0)),
        ],
        out_specs=pl.BlockSpec((chunk * lon_cells, lat_cells), lambda n: (n, 0)),
        scratch_shapes=[
            pltpu.VMEM((lon_cells + 2, width, lat_cells), F32),
            pltpu.VMEM((3 * width, lon_cells * lat_cells), BF16),
        ],
        compiler_params=pltpu.CompilerParams(vmem_limit_bytes=40 * 2**20),
    )(*parts, center, neighbor)
    return out.reshape(extent, lon_cells, lat_cells)


def on_device(*arrays):
    rows, width = arrays[0].shape
    lon_n = lax.axis_size("lon")
    fits = 2 * rows // lon_n == 128 and width == 128 and arrays[6].shape == (16, 128) and lon_n <= 16
    return (fast if fits else plain)(*arrays)


def solution(mesh):
    return jax.shard_map(
        on_device,
        mesh=mesh,
        in_specs=(
            P(("lon", "lat"), None),
            P(("lon", "lat"), None),
            P(("lon", "lat")),
            P(("lon", "lat")),
            P(),
            P(),
            P("lon", "lat"),
            P(None, "lon", "lat"),
        ),
        out_specs=P(None, "lon", "lat"),
        check_vma=False,
    )
```

```python
import functools

import jax
import jax.numpy as jnp
from jax import lax
from jax.experimental import pallas as pl
from jax.experimental.pallas import tpu as pltpu
from jax.sharding import PartitionSpec as P

STEPS = 2
MESH = pl.DeviceIdType.MESH
HIGHEST = lax.Precision.HIGHEST
NT = (((1,), (1,)), ((), ()))
BF16 = jnp.bfloat16
F32 = jnp.float32


def with_halo(x, sides, width, wrap):
    for axis, dim in sides:
        size, length = (lax.axis_size(axis), x.shape[dim])
        up = [(i, (i + 1) % size) for i in range(size if wrap else size - 1)]
        down = [(j, i) for i, j in up]
        last = lax.slice_in_dim(x, length - width, length, axis=dim)
        first = lax.slice_in_dim(x, 0, width, axis=dim)
        before = lax.ppermute(last, axis, up)
        after = lax.ppermute(first, axis, down)
        x = jnp.concatenate([before, x, after], axis=dim)
    return x


def stencil(spread, middle, weights):
    return (
        middle * spread[:, 1:-1, 1:-1]
        + weights[0] * spread[:, :-2, 1:-1]
        + weights[1] * spread[:, 2:, 1:-1]
        + weights[2] * spread[:, 1:-1, :-2]
        + weights[3] * spread[:, 1:-1, 2:]
    )


def plain(obs_values, obs_owner, obs_cell, obs_count, obs_map, column_mix, center, neighbor):
    lon_count = lax.axis_size("lon")
    rows, width = obs_values.shape
    capacity = 2 * rows // lon_count
    slots = lon_count * capacity
    lon_cells, lat_cells = center.shape
    owners = obs_owner[:, 0]
    living = jnp.arange(rows, dtype=jnp.int32) < obs_count[0]
    number = jnp.arange(rows, dtype=jnp.int32)
    same = (owners[:, None] == owners[None, :]) & (number[None, :] < number[:, None])
    earlier = jnp.sum(same.astype(jnp.int32), axis=1)
    target = jnp.where(living, owners * capacity + earlier, -1)
    chosen = jnp.arange(slots, dtype=jnp.int32)[:, None] == target[None, :]
    packed = jnp.dot(chosen.astype(BF16), obs_values, preferred_element_type=F32).astype(BF16)
    places = jnp.sum(jnp.where(chosen, obs_cell[None, :] + 1, 0), axis=1) - 1
    packed = packed.reshape(lon_count, capacity, width)
    places = places.reshape(lon_count, capacity)
    packed = lax.all_to_all(packed, "lon", split_axis=0, concat_axis=0, tiled=True)
    places = lax.all_to_all(places, "lon", split_axis=0, concat_axis=0, tiled=True)
    cells = jnp.arange(lon_cells * lat_cells, dtype=jnp.int32)
    onehot = (places.reshape(slots)[:, None] == cells[None, :]).astype(BF16)
    adjoint = lax.dot_general(
        packed.reshape(slots, width), onehot, (((0,), (0,)), ((), ())), preferred_element_type=F32
    ).reshape(width, lon_cells, lat_cells)
    weight = obs_map.astype(F32)
    for section in range(STEPS):
        weight = jnp.dot(weight, column_mix, precision=HIGHEST)
        spread = with_halo(adjoint, (("lon", 1),), 1, True)
        spread = with_halo(spread, (("lat", 2),), 1, False)
        adjoint = stencil(spread, center, neighbor)
    return jnp.einsum("vb,vij->bij", weight, adjoint, precision=HIGHEST)


def iota(shape, dim):
    return lax.broadcasted_iota(jnp.int32, shape, dim)


def onehot_of(labels, count):
    return jnp.where(iota((count, labels.shape[1]), 0) == labels, 1.0, 0.0).astype(BF16)


def route_kernel(
    lon_n, lat_n,
    values_in, owner_in, cell_in, count, obs_map_in, mix_in, center_in, neighbor_in,
    f_out, halo_out, edge_out, corner_out, wlon_out, wlat_out, weight_out,
    send, recv, fsend, halo, esend, edge, corner, wlon_send, wlon, wlat_send, wlat,
    a_send, a_recv, h_send, h_recv,
    values, owner, cell, obs_map, mix, center, neighbor, in_sem,
):
    pairs_in = [
        (owner_in, owner), (cell_in, cell), (values_in, values), (center_in, center),
        (neighbor_in, neighbor), (obs_map_in, obs_map), (mix_in, mix),
    ]
    fetches = [pltpu.make_async_copy(a, b, in_sem.at[n]) for n, (a, b) in enumerate(pairs_in)]
    for fetch in fetches:
        fetch.start()
    me, band = lax.axis_index("lon"), lax.axis_index("lat")
    east, west = lax.rem(me + 1, lon_n), lax.rem(me + lon_n - 1, lon_n)
    north, south = lax.rem(band + 1, lat_n), lax.rem(band + lat_n - 1, lat_n)
    barrier = pltpu.get_barrier_semaphore()
    partners = [(lax.rem(me + k, lon_n), band) for k in range(1, lon_n)]
    partners += [(a, b) for a in (me, east, west) for b in (north, south)]
    for partner in partners:
        pl.semaphore_signal(barrier, inc=1, device_id=partner, device_id_type=MESH)

    lon_cells, lat_cells = center.shape
    rows, width = values.shape
    cap = 2 * rows // lon_n
    for fetch in fetches[:3]:
        fetch.wait()
    own, place = owner[...], cell[...]
    owned = iota((16, rows), 0) == own
    before = jnp.where(iota((rows, rows), 0) < iota((rows, rows), 1), 1.0, 0.0).astype(BF16)
    prior = jnp.dot(jnp.where(owned, 1.0, 0.0).astype(BF16), before, preferred_element_type=F32)
    position = jnp.sum(jnp.where(owned, prior, 0.0), axis=0, keepdims=True).astype(jnp.int32)
    target = jnp.where(iota((1, rows), 1) < count[0], own * cap + position, -1)
    chosen = onehot_of(target, lon_n * cap)
    i, j = place // lat_cells, place % lat_cells
    side = jnp.where(j < 2, j, jnp.where(j >= lat_cells - 2, j - (lat_cells - 4), 4))
    sub = iota((16, rows), 0)
    labels = jnp.where(
        sub == 0,
        i // 2,
        jnp.where(sub == 1, (i % 2) * lat_cells + j, jnp.where(sub == 2, side * lon_cells + i, 0)),
    ).astype(F32)
    turned = jnp.concatenate([values[...].astype(F32).T, labels], axis=0).astype(BF16)
    packed = lax.dot_general(turned, chosen, NT, preferred_element_type=F32).astype(BF16)
    for o in range(lon_n):
        send[o] = packed[:, o * cap : (o + 1) * cap]

    for fetch in fetches[3:5]:
        fetch.wait()
    weights = [center[...]] + [neighbor[k] for k in range(4)]
    wlon_send[...] = jnp.zeros_like(wlon_send)
    for k in range(5):
        wlon_send[0, k : k + 1, :] = weights[k][0:1]
        wlon_send[1, k : k + 1, :] = weights[k][lon_cells - 1 : lon_cells]
    stacked = jnp.concatenate(weights + [jnp.zeros((128 - 5 * lon_cells, lat_cells), F32)], axis=0).T
    wlat_send[0] = stacked[0:8]
    wlat_send[1] = stacked[lat_cells - 8 : lat_cells]

    pl.semaphore_wait(barrier, len(partners))

    def copy(src, dst, sem_out, sem_in, device):
        return pltpu.make_async_remote_copy(
            src_ref=src, dst_ref=dst, send_sem=sem_out, recv_sem=sem_in,
            device_id=device, device_id_type=MESH,
        )

    moves = []
    for k in range(1, lon_n):
        to = lax.rem(me + k, lon_n)
        moves.append(copy(send.at[to], recv.at[k], a_send.at[k - 1], a_recv.at[k - 1], (to, band)))
        moves[-1].start()
    later = []

    def start_later(src, dst, device):
        n = len(later)
        later.append(copy(src, dst, h_send.at[n], h_recv.at[n], device))
        later[-1].start()

    start_later(wlon_send.at[1], wlon.at[0], (east, band))
    start_later(wlon_send.at[0], wlon.at[1], (west, band))
    start_later(wlat_send.at[1], wlat.at[0], (me, north))
    start_later(wlat_send.at[0], wlat.at[1], (me, south))
    recv[0] = send[me]

    for fetch in fetches[5:]:
        fetch.wait()
    weight = obs_map[...].astype(F32)
    for section in range(STEPS):
        weight = jnp.dot(weight, mix[...], precision=HIGHEST, preferred_element_type=F32)
    weight = weight.T
    high = weight.astype(BF16)
    low = (weight - high.astype(F32)).astype(BF16)
    weight_out[...] = jnp.concatenate([high, high, low], axis=1)

    for move in moves:
        move.wait()

    arrived = jnp.concatenate([recv[k, 0:width, :] for k in range(lon_n)], axis=1)
    marks = jnp.concatenate([recv[k, width : width + 16, :] for k in range(lon_n)], axis=1)
    marks = marks.astype(F32).astype(jnp.int32)
    pair, column, rim = marks[0:1], marks[1:2], marks[2:3]
    columns = onehot_of(column, 2 * lat_cells)

    def masked(p):
        return arrived * jnp.where(pair == p, 1.0, 0.0).astype(BF16)

    def spread(pairs):
        left = jnp.concatenate([masked(p) for p in pairs], axis=0)
        out = lax.dot_general(left, columns, NT, preferred_element_type=F32).astype(BF16)
        for n, p in enumerate(pairs):
            for half in range(2):
                yield 2 * p + half, out[n * width : (n + 1) * width, half * lat_cells : (half + 1) * lat_cells]

    pairs = lon_cells // 2
    for n, (at, block) in enumerate(spread((0, pairs - 1))):
        fsend[n] = block
        f_out[at] = block
    start_later(fsend.at[pl.ds(2, 2)], halo.at[pl.ds(0, 2)], (east, band))
    start_later(fsend.at[pl.ds(0, 2)], halo.at[pl.ds(2, 2)], (west, band))
    rims = onehot_of(rim, 4 * lon_cells)
    esend[...] = lax.dot_general(rims, arrived, NT, preferred_element_type=F32).astype(BF16)
    start_later(esend.at[pl.ds(32, 32)], edge.at[pl.ds(0, 32)], (me, north))
    start_later(esend.at[pl.ds(0, 32)], edge.at[pl.ds(32, 32)], (me, south))
    start_later(esend.at[pl.ds(48, 16)], corner.at[0], (east, north))
    start_later(esend.at[pl.ds(0, 16)], corner.at[1], (east, south))
    start_later(esend.at[pl.ds(48, 16)], corner.at[2], (west, north))
    start_later(esend.at[pl.ds(0, 16)], corner.at[3], (west, south))
    for at, block in spread(range(1, pairs - 1)):
        f_out[at] = block
    for move in later:
        move.wait()
    halo_out[...] = halo[...]
    edge_out[0:64] = edge[...]
    edge_out[64:80] = esend[0:16]
    edge_out[80:96] = esend[48:64]
    corner_out[...] = corner[...]
    wlon_out[...] = wlon[...]
    wlat_out[...] = wlat[...]


def apply_kernel(
    lat_n, f, halo, edge, corner, wlon, wlat, weight, center, neighbor, out, first, grid_values
):
    lon_cells, lat_cells = center.shape
    width = f.shape[1]

    @pl.when(pl.program_id(0) == 0)
    def _():
        band = lax.axis_index("lat")
        keeps = [jnp.where(band > 0, 1.0, 0.0), jnp.where(band < lat_n - 1, 1.0, 0.0)]
        rim = edge[...].astype(F32)
        south2, south1, north1, north2, inner_s, inner_n = (rim[16 * n : 16 * (n + 1)] for n in range(6))
        corners = corner[...].astype(F32)
        cws, cwn, ces, cen = corners[0, 15:16], corners[1, 15:16], corners[2, 0:1], corners[3, 0:1]

        def rim_step(turned, here, west, east, below, above):
            w = [turned[16 * k : 16 * (k + 1)] for k in range(5)]
            up = jnp.concatenate([west, here[:-1]], axis=0)
            down = jnp.concatenate([here[1:], east], axis=0)
            return w[0] * here + w[1] * up + w[2] * down + w[3] * below + w[4] * above

        tall = jnp.zeros((120, 128), F32)
        ws = jnp.concatenate([wlat[0], tall], axis=0).T[:, 7:8]
        wn = jnp.concatenate([wlat[1], tall], axis=0).T[:, 0:1]
        step_s = rim_step(ws, south1, cws, ces, south2, inner_s)
        step_n = rim_step(wn, north1, cwn, cen, inner_n, north2)
        table = jnp.concatenate(
            [south1 * keeps[0], north1 * keeps[1], step_s * keeps[0], step_n * keeps[1],
             cws * keeps[0], cwn * keeps[1], ces * keeps[0], cen * keeps[1],
             jnp.zeros((60, width), F32)], axis=0,
        ).T
        lane = iota((width, lat_cells), 1)

        def value(n):
            if n < 0:
                return halo[n + 2].astype(F32)
            return halo[n - lon_cells + 2].astype(F32) if n >= lon_cells else f[n].astype(F32)

        def weights_at(n):
            if n < 0:
                return [wlon[0, k : k + 1, :] for k in range(5)]
            if n >= lon_cells:
                return [wlon[1, k : k + 1, :] for k in range(5)]
            return [center[n : n + 1, :]] + [neighbor[k, n : n + 1, :] for k in range(4)]

        def step(n, here, west, east, s, t):
            w = weights_at(n)
            below = jnp.where(lane == 0, table[:, s : s + 1], pltpu.roll(here, 1, 1))
            above = jnp.where(lane == lat_cells - 1, table[:, t : t + 1], pltpu.roll(here, lat_cells - 1, 1))
            return w[0] * here + w[1] * west + w[2] * east + w[3] * below + w[4] * above

        for n in range(-1, lon_cells + 1):
            s, t = (64, 65) if n < 0 else (66, 67) if n >= lon_cells else (n, 16 + n)
            first[n + 1] = step(n, value(n), value(n - 1), value(n + 1), s, t)
        for n in range(lon_cells):
            done = step(n, first[n + 1], first[n], first[n + 2], 32 + n, 48 + n)
            high = done.astype(BF16)
            at = slice(n * lat_cells, (n + 1) * lat_cells)
            grid_values[0:width, at] = high
            grid_values[width : 2 * width, at] = (done - high.astype(F32)).astype(BF16)
            grid_values[2 * width : 3 * width, at] = high

    result = jnp.dot(weight[...], grid_values[...], preferred_element_type=F32)
    chunk = weight.shape[0]
    for n in range(lon_cells):
        out[pl.ds(n, chunk, stride=lon_cells), :] = result[:, n * lat_cells : (n + 1) * lat_cells]


def fast(obs_values, obs_owner, obs_cell, obs_count, obs_map, column_mix, center, neighbor):
    lon_n, lat_n = lax.axis_size("lon"), lax.axis_size("lat")
    rows, width = obs_values.shape
    extent = column_mix.shape[0]
    lon_cells, lat_cells = center.shape
    cap = 2 * rows // lon_n
    vmem, shape = pl.BlockSpec(memory_space=pltpu.VMEM), jax.ShapeDtypeStruct
    hbm = pl.BlockSpec(memory_space=pltpu.HBM)
    parts = pl.pallas_call(
        functools.partial(route_kernel, lon_n, lat_n),
        out_shape=[
            shape((lon_cells, width, lat_cells), BF16),
            shape((4, width, lat_cells), BF16),
            shape((96, width), BF16),
            shape((4, 16, width), BF16),
            shape((2, 8, lat_cells), F32),
            shape((2, 8, 128), F32),
            shape((extent, 3 * width), BF16),
        ],
        in_specs=[hbm] * 3 + [pl.BlockSpec(memory_space=pltpu.SMEM)] + [hbm] * 4,
        out_specs=[vmem] * 7,
        scratch_shapes=[
            pltpu.VMEM((lon_n, width + 16, cap), BF16),
            pltpu.VMEM((lon_n, width + 16, cap), BF16),
            pltpu.VMEM((4, width, lat_cells), BF16),
            pltpu.VMEM((4, width, lat_cells), BF16),
            pltpu.VMEM((64, width), BF16),
            pltpu.VMEM((64, width), BF16),
            pltpu.VMEM((4, 16, width), BF16),
            pltpu.VMEM((2, 8, lat_cells), F32),
            pltpu.VMEM((2, 8, lat_cells), F32),
            pltpu.VMEM((2, 8, 128), F32),
            pltpu.VMEM((2, 8, 128), F32),
            pltpu.SemaphoreType.DMA((lon_n - 1,)),
            pltpu.SemaphoreType.DMA((lon_n - 1,)),
            pltpu.SemaphoreType.DMA((12,)),
            pltpu.SemaphoreType.DMA((12,)),
            pltpu.VMEM(obs_values.shape, BF16),
            pltpu.VMEM((1, rows), jnp.int32),
            pltpu.VMEM((1, rows), jnp.int32),
            pltpu.VMEM(obs_map.shape, BF16),
            pltpu.VMEM(column_mix.shape, F32),
            pltpu.VMEM(center.shape, F32),
            pltpu.VMEM(neighbor.shape, F32),
            pltpu.SemaphoreType.DMA((7,)),
        ],
        compiler_params=pltpu.CompilerParams(
            collective_id=0, has_side_effects=True, vmem_limit_bytes=62 * 2**20
        ),
    )(obs_values, obs_owner.reshape(1, rows), obs_cell.reshape(1, rows), obs_count, obs_map, column_mix, center, neighbor)
    chunk = extent // 6
    whole = [pl.BlockSpec(x.shape, functools.partial(lambda d, n: (0,) * d, x.ndim)) for x in parts[:6]]
    out = pl.pallas_call(
        functools.partial(apply_kernel, lat_n),
        grid=(extent // chunk,),
        out_shape=shape((extent * lon_cells, lat_cells), F32),
        in_specs=whole + [
            pl.BlockSpec((chunk, 3 * width), lambda n: (n, 0)),
            pl.BlockSpec(center.shape, lambda n: (0, 0)),
            pl.BlockSpec(neighbor.shape, lambda n: (0, 0, 0)),
        ],
        out_specs=pl.BlockSpec((chunk * lon_cells, lat_cells), lambda n: (n, 0)),
        scratch_shapes=[
            pltpu.VMEM((lon_cells + 2, width, lat_cells), F32),
            pltpu.VMEM((3 * width, lon_cells * lat_cells), BF16),
        ],
        compiler_params=pltpu.CompilerParams(vmem_limit_bytes=62 * 2**20),
    )(*parts, center, neighbor)
    return out.reshape(extent, lon_cells, lat_cells)


def on_device(*arrays):
    rows, width = arrays[0].shape
    lon_n = lax.axis_size("lon")
    fits = 2 * rows // lon_n == 128 and width == 128 and arrays[6].shape == (16, 128) and lon_n <= 16
    return (fast if fits else plain)(*arrays)


def solution(mesh):
    return jax.shard_map(
        on_device,
        mesh=mesh,
        in_specs=(
            P(("lon", "lat"), None),
            P(("lon", "lat"), None),
            P(("lon", "lat")),
            P(("lon", "lat")),
            P(),
            P(),
            P("lon", "lat"),
            P(None, "lon", "lat"),
        ),
        out_specs=P(None, "lon", "lat"),
        check_vma=False,
    )
```

```python
import functools

import jax
import jax.numpy as jnp
from jax import lax
from jax.experimental import pallas as pl
from jax.experimental.pallas import tpu as pltpu
from jax.sharding import PartitionSpec as P

STEPS = 2
MESH = pl.DeviceIdType.MESH
HIGHEST = lax.Precision.HIGHEST
NT = (((1,), (1,)), ((), ()))
BF16 = jnp.bfloat16
F32 = jnp.float32


def with_halo(x, sides, width, wrap):
    for axis, dim in sides:
        size, length = (lax.axis_size(axis), x.shape[dim])
        up = [(i, (i + 1) % size) for i in range(size if wrap else size - 1)]
        down = [(j, i) for i, j in up]
        last = lax.slice_in_dim(x, length - width, length, axis=dim)
        first = lax.slice_in_dim(x, 0, width, axis=dim)
        before = lax.ppermute(last, axis, up)
        after = lax.ppermute(first, axis, down)
        x = jnp.concatenate([before, x, after], axis=dim)
    return x


def stencil(spread, middle, weights):
    return (
        middle * spread[:, 1:-1, 1:-1]
        + weights[0] * spread[:, :-2, 1:-1]
        + weights[1] * spread[:, 2:, 1:-1]
        + weights[2] * spread[:, 1:-1, :-2]
        + weights[3] * spread[:, 1:-1, 2:]
    )


def plain(obs_values, obs_owner, obs_cell, obs_count, obs_map, column_mix, center, neighbor):
    lon_count = lax.axis_size("lon")
    rows, width = obs_values.shape
    capacity = 2 * rows // lon_count
    slots = lon_count * capacity
    lon_cells, lat_cells = center.shape
    owners = obs_owner[:, 0]
    living = jnp.arange(rows, dtype=jnp.int32) < obs_count[0]
    number = jnp.arange(rows, dtype=jnp.int32)
    same = (owners[:, None] == owners[None, :]) & (number[None, :] < number[:, None])
    earlier = jnp.sum(same.astype(jnp.int32), axis=1)
    target = jnp.where(living, owners * capacity + earlier, -1)
    chosen = jnp.arange(slots, dtype=jnp.int32)[:, None] == target[None, :]
    packed = jnp.dot(chosen.astype(BF16), obs_values, preferred_element_type=F32).astype(BF16)
    places = jnp.sum(jnp.where(chosen, obs_cell[None, :] + 1, 0), axis=1) - 1
    packed = packed.reshape(lon_count, capacity, width)
    places = places.reshape(lon_count, capacity)
    packed = lax.all_to_all(packed, "lon", split_axis=0, concat_axis=0, tiled=True)
    places = lax.all_to_all(places, "lon", split_axis=0, concat_axis=0, tiled=True)
    cells = jnp.arange(lon_cells * lat_cells, dtype=jnp.int32)
    onehot = (places.reshape(slots)[:, None] == cells[None, :]).astype(BF16)
    adjoint = lax.dot_general(
        packed.reshape(slots, width), onehot, (((0,), (0,)), ((), ())), preferred_element_type=F32
    ).reshape(width, lon_cells, lat_cells)
    weight = obs_map.astype(F32)
    for section in range(STEPS):
        weight = jnp.dot(weight, column_mix, precision=HIGHEST)
        spread = with_halo(adjoint, (("lon", 1),), 1, True)
        spread = with_halo(spread, (("lat", 2),), 1, False)
        adjoint = stencil(spread, center, neighbor)
    return jnp.einsum("vb,vij->bij", weight, adjoint, precision=HIGHEST)


def iota(shape, dim):
    return lax.broadcasted_iota(jnp.int32, shape, dim)


def onehot_of(labels, count):
    return jnp.where(iota((count, labels.shape[1]), 0) == labels, 1.0, 0.0).astype(BF16)


def route_kernel(
    lon_n, lat_n,
    values_in, owner_in, cell_in, count, obs_map_in, mix_in, center_in, neighbor_in,
    f_out, halo_out, edge_out, corner_out, wlon_out, wlat_out, weight_out,
    send, recv, fsend, halo, esend, edge, corner, wlon_send, wlon, wlat_send, wlat,
    a_send, a_recv, h_send, h_recv,
    values, owner, cell, obs_map, mix, center, neighbor, in_sem,
):
    pairs_in = [
        (owner_in, owner), (cell_in, cell), (values_in, values), (center_in, center),
        (neighbor_in, neighbor), (obs_map_in, obs_map), (mix_in, mix),
    ]
    fetches = [pltpu.make_async_copy(a, b, in_sem.at[n]) for n, (a, b) in enumerate(pairs_in)]
    for fetch in fetches:
        fetch.start()
    me, band = lax.axis_index("lon"), lax.axis_index("lat")
    east, west = lax.rem(me + 1, lon_n), lax.rem(me + lon_n - 1, lon_n)
    north, south = lax.rem(band + 1, lat_n), lax.rem(band + lat_n - 1, lat_n)
    barrier = pltpu.get_barrier_semaphore()
    partners = [(lax.rem(me + k, lon_n), band) for k in range(1, lon_n)]
    partners += [(a, b) for a in (me, east, west) for b in (north, south)]
    for partner in partners:
        pl.semaphore_signal(barrier, inc=1, device_id=partner, device_id_type=MESH)

    lon_cells, lat_cells = center.shape
    rows, width = values.shape
    cap = 2 * rows // lon_n
    for fetch in fetches[:3]:
        fetch.wait()
    own, place = owner[...], cell[...]
    owned = iota((16, rows), 0) == own
    before = jnp.where(iota((rows, rows), 0) < iota((rows, rows), 1), 1.0, 0.0).astype(BF16)
    prior = jnp.dot(jnp.where(owned, 1.0, 0.0).astype(BF16), before, preferred_element_type=F32)
    position = jnp.sum(jnp.where(owned, prior, 0.0), axis=0, keepdims=True).astype(jnp.int32)
    target = jnp.where(iota((1, rows), 1) < count[0], own * cap + position, -1)
    chosen = onehot_of(target, lon_n * cap)
    i, j = place // lat_cells, place % lat_cells
    side = jnp.where(j < 2, j, jnp.where(j >= lat_cells - 2, j - (lat_cells - 4), 4))
    sub = iota((16, rows), 0)
    labels = jnp.where(
        sub == 0,
        i // 2,
        jnp.where(sub == 1, (i % 2) * lat_cells + j, jnp.where(sub == 2, side * lon_cells + i, 0)),
    ).astype(F32)
    turned = jnp.concatenate([values[...].astype(F32).T, labels], axis=0).astype(BF16)
    packed = lax.dot_general(turned, chosen, NT, preferred_element_type=F32).astype(BF16)
    for o in range(lon_n):
        send[o] = packed[:, o * cap : (o + 1) * cap]

    for fetch in fetches[3:5]:
        fetch.wait()
    weights = [center[...]] + [neighbor[k] for k in range(4)]
    wlon_send[...] = jnp.zeros_like(wlon_send)
    for k in range(5):
        wlon_send[0, k : k + 1, :] = weights[k][0:1]
        wlon_send[1, k : k + 1, :] = weights[k][lon_cells - 1 : lon_cells]
    stacked = jnp.concatenate(weights + [jnp.zeros((128 - 5 * lon_cells, lat_cells), F32)], axis=0).T
    wlat_send[0] = stacked[0:8]
    wlat_send[1] = stacked[lat_cells - 8 : lat_cells]

    pl.semaphore_wait(barrier, len(partners))

    def copy(src, dst, sem_out, sem_in, device):
        return pltpu.make_async_remote_copy(
            src_ref=src, dst_ref=dst, send_sem=sem_out, recv_sem=sem_in,
            device_id=device, device_id_type=MESH,
        )

    moves = []
    for k in range(1, lon_n):
        to = lax.rem(me + k, lon_n)
        moves.append(copy(send.at[to], recv.at[k], a_send.at[k - 1], a_recv.at[k - 1], (to, band)))
        moves[-1].start()
    later = []

    def start_later(src, dst, device):
        n = len(later)
        later.append(copy(src, dst, h_send.at[n], h_recv.at[n], device))
        later[-1].start()

    start_later(wlon_send.at[1], wlon.at[0], (east, band))
    start_later(wlon_send.at[0], wlon.at[1], (west, band))
    start_later(wlat_send.at[1], wlat.at[0], (me, north))
    start_later(wlat_send.at[0], wlat.at[1], (me, south))
    recv[0] = send[me]

    for fetch in fetches[5:]:
        fetch.wait()
    weight = obs_map[...].astype(F32)
    for section in range(STEPS):
        weight = jnp.dot(weight, mix[...], precision=HIGHEST, preferred_element_type=F32)
    weight = weight.T
    high = weight.astype(BF16)
    low = (weight - high.astype(F32)).astype(BF16)
    weight_out[...] = jnp.concatenate([high, high, low], axis=1)

    for move in moves:
        move.wait()

    arrived = jnp.concatenate([recv[k, 0:width, :] for k in range(lon_n)], axis=1)
    marks = jnp.concatenate([recv[k, width : width + 16, :] for k in range(lon_n)], axis=1)
    marks = marks.astype(F32).astype(jnp.int32)
    pair, column, rim = marks[0:1], marks[1:2], marks[2:3]
    columns = onehot_of(column, 2 * lat_cells)

    def masked(p):
        return arrived * jnp.where(pair == p, 1.0, 0.0).astype(BF16)

    def spread(pairs):
        left = jnp.concatenate([masked(p) for p in pairs], axis=0)
        out = lax.dot_general(left, columns, NT, preferred_element_type=F32).astype(BF16)
        for n, p in enumerate(pairs):
            for half in range(2):
                yield 2 * p + half, out[n * width : (n + 1) * width, half * lat_cells : (half + 1) * lat_cells]

    pairs = lon_cells // 2
    for n, (at, block) in enumerate(spread((0, pairs - 1))):
        fsend[n] = block
        f_out[at] = block
    start_later(fsend.at[pl.ds(2, 2)], halo.at[pl.ds(0, 2)], (east, band))
    start_later(fsend.at[pl.ds(0, 2)], halo.at[pl.ds(2, 2)], (west, band))
    rims = onehot_of(rim, 4 * lon_cells)
    esend[...] = lax.dot_general(rims, arrived, NT, preferred_element_type=F32).astype(BF16)
    start_later(esend.at[pl.ds(32, 32)], edge.at[pl.ds(0, 32)], (me, north))
    start_later(esend.at[pl.ds(0, 32)], edge.at[pl.ds(32, 32)], (me, south))
    start_later(esend.at[pl.ds(48, 16)], corner.at[0], (east, north))
    start_later(esend.at[pl.ds(0, 16)], corner.at[1], (east, south))
    start_later(esend.at[pl.ds(48, 16)], corner.at[2], (west, north))
    start_later(esend.at[pl.ds(0, 16)], corner.at[3], (west, south))
    for at, block in spread(range(1, pairs - 1)):
        f_out[at] = block
    for move in later:
        move.wait()
    halo_out[...] = halo[...]
    edge_out[0:64] = edge[...]
    edge_out[64:80] = esend[0:16]
    edge_out[80:96] = esend[48:64]
    corner_out[...] = corner[...]
    wlon_out[...] = wlon[...]
    wlat_out[...] = wlat[...]


def apply_kernel(
    lat_n, f, halo, edge, corner, wlon, wlat, weight, center, neighbor, out, first, grid_values
):
    lon_cells, lat_cells = center.shape
    width = f.shape[1]

    @pl.when(pl.program_id(0) == 0)
    def _():
        band = lax.axis_index("lat")
        keeps = [jnp.where(band > 0, 1.0, 0.0), jnp.where(band < lat_n - 1, 1.0, 0.0)]
        rim = edge[...].astype(F32)
        south2, south1, north1, north2, inner_s, inner_n = (rim[16 * n : 16 * (n + 1)] for n in range(6))
        corners = corner[...].astype(F32)
        cws, cwn, ces, cen = corners[0, 15:16], corners[1, 15:16], corners[2, 0:1], corners[3, 0:1]

        def rim_step(turned, here, west, east, below, above):
            w = [turned[16 * k : 16 * (k + 1)] for k in range(5)]
            up = jnp.concatenate([west, here[:-1]], axis=0)
            down = jnp.concatenate([here[1:], east], axis=0)
            return w[0] * here + w[1] * up + w[2] * down + w[3] * below + w[4] * above

        tall = jnp.zeros((120, 128), F32)
        ws = jnp.concatenate([wlat[0], tall], axis=0).T[:, 7:8]
        wn = jnp.concatenate([wlat[1], tall], axis=0).T[:, 0:1]
        step_s = rim_step(ws, south1, cws, ces, south2, inner_s)
        step_n = rim_step(wn, north1, cwn, cen, inner_n, north2)
        table = jnp.concatenate(
            [south1 * keeps[0], north1 * keeps[1], step_s * keeps[0], step_n * keeps[1],
             cws * keeps[0], cwn * keeps[1], ces * keeps[0], cen * keeps[1],
             jnp.zeros((60, width), F32)], axis=0,
        ).T
        lane = iota((width, lat_cells), 1)

        def value(n):
            if n < 0:
                return halo[n + 2].astype(F32)
            return halo[n - lon_cells + 2].astype(F32) if n >= lon_cells else f[n].astype(F32)

        def weights_at(n):
            if n < 0:
                return [wlon[0, k : k + 1, :] for k in range(5)]
            if n >= lon_cells:
                return [wlon[1, k : k + 1, :] for k in range(5)]
            return [center[n : n + 1, :]] + [neighbor[k, n : n + 1, :] for k in range(4)]

        def step(n, here, west, east, s, t):
            w = weights_at(n)
            below = jnp.where(lane == 0, table[:, s : s + 1], pltpu.roll(here, 1, 1))
            above = jnp.where(lane == lat_cells - 1, table[:, t : t + 1], pltpu.roll(here, lat_cells - 1, 1))
            return w[0] * here + w[1] * west + w[2] * east + w[3] * below + w[4] * above

        for n in range(-1, lon_cells + 1):
            s, t = (64, 65) if n < 0 else (66, 67) if n >= lon_cells else (n, 16 + n)
            first[n + 1] = step(n, value(n), value(n - 1), value(n + 1), s, t)
        for n in range(lon_cells):
            done = step(n, first[n + 1], first[n], first[n + 2], 32 + n, 48 + n)
            high = done.astype(BF16)
            at = slice(n * lat_cells, (n + 1) * lat_cells)
            grid_values[0:width, at] = high
            grid_values[width : 2 * width, at] = (done - high.astype(F32)).astype(BF16)
            grid_values[2 * width : 3 * width, at] = high

    result = jnp.dot(weight[...], grid_values[...], preferred_element_type=F32)
    chunk = weight.shape[0]
    for n in range(lon_cells):
        out[pl.ds(n, chunk, stride=lon_cells), :] = result[:, n * lat_cells : (n + 1) * lat_cells]


def fast(obs_values, obs_owner, obs_cell, obs_count, obs_map, column_mix, center, neighbor):
    lon_n, lat_n = lax.axis_size("lon"), lax.axis_size("lat")
    rows, width = obs_values.shape
    extent = column_mix.shape[0]
    lon_cells, lat_cells = center.shape
    cap = 2 * rows // lon_n
    vmem, shape = pl.BlockSpec(memory_space=pltpu.VMEM), jax.ShapeDtypeStruct
    hbm = pl.BlockSpec(memory_space=pltpu.HBM)
    parts = pl.pallas_call(
        functools.partial(route_kernel, lon_n, lat_n),
        out_shape=[
            shape((lon_cells, width, lat_cells), BF16),
            shape((4, width, lat_cells), BF16),
            shape((96, width), BF16),
            shape((4, 16, width), BF16),
            shape((2, 8, lat_cells), F32),
            shape((2, 8, 128), F32),
            shape((extent, 3 * width), BF16),
        ],
        in_specs=[hbm] * 3 + [pl.BlockSpec(memory_space=pltpu.SMEM)] + [hbm] * 4,
        out_specs=[vmem] * 7,
        scratch_shapes=[
            pltpu.VMEM((lon_n, width + 16, cap), BF16),
            pltpu.VMEM((lon_n, width + 16, cap), BF16),
            pltpu.VMEM((4, width, lat_cells), BF16),
            pltpu.VMEM((4, width, lat_cells), BF16),
            pltpu.VMEM((64, width), BF16),
            pltpu.VMEM((64, width), BF16),
            pltpu.VMEM((4, 16, width), BF16),
            pltpu.VMEM((2, 8, lat_cells), F32),
            pltpu.VMEM((2, 8, lat_cells), F32),
            pltpu.VMEM((2, 8, 128), F32),
            pltpu.VMEM((2, 8, 128), F32),
            pltpu.SemaphoreType.DMA((lon_n - 1,)),
            pltpu.SemaphoreType.DMA((lon_n - 1,)),
            pltpu.SemaphoreType.DMA((12,)),
            pltpu.SemaphoreType.DMA((12,)),
            pltpu.VMEM(obs_values.shape, BF16),
            pltpu.VMEM((1, rows), jnp.int32),
            pltpu.VMEM((1, rows), jnp.int32),
            pltpu.VMEM(obs_map.shape, BF16),
            pltpu.VMEM(column_mix.shape, F32),
            pltpu.VMEM(center.shape, F32),
            pltpu.VMEM(neighbor.shape, F32),
            pltpu.SemaphoreType.DMA((7,)),
        ],
        compiler_params=pltpu.CompilerParams(
            collective_id=0, has_side_effects=True, vmem_limit_bytes=62 * 2**20
        ),
    )(obs_values, obs_owner.reshape(1, rows), obs_cell.reshape(1, rows), obs_count, obs_map, column_mix, center, neighbor)
    chunk = extent // 3
    whole = [pl.BlockSpec(x.shape, functools.partial(lambda d, n: (0,) * d, x.ndim)) for x in parts[:6]]
    out = pl.pallas_call(
        functools.partial(apply_kernel, lat_n),
        grid=(extent // chunk,),
        out_shape=shape((extent * lon_cells, lat_cells), F32),
        in_specs=whole + [
            pl.BlockSpec((chunk, 3 * width), lambda n: (n, 0)),
            pl.BlockSpec(center.shape, lambda n: (0, 0)),
            pl.BlockSpec(neighbor.shape, lambda n: (0, 0, 0)),
        ],
        out_specs=pl.BlockSpec((chunk * lon_cells, lat_cells), lambda n: (n, 0)),
        scratch_shapes=[
            pltpu.VMEM((lon_cells + 2, width, lat_cells), F32),
            pltpu.VMEM((3 * width, lon_cells * lat_cells), BF16),
        ],
        compiler_params=pltpu.CompilerParams(vmem_limit_bytes=62 * 2**20),
    )(*parts, center, neighbor)
    return out.reshape(extent, lon_cells, lat_cells)


def on_device(*arrays):
    rows, width = arrays[0].shape
    lon_n = lax.axis_size("lon")
    fits = 2 * rows // lon_n == 128 and width == 128 and arrays[6].shape == (16, 128) and lon_n <= 16
    return (fast if fits else plain)(*arrays)


def solution(mesh):
    return jax.shard_map(
        on_device,
        mesh=mesh,
        in_specs=(
            P(("lon", "lat"), None),
            P(("lon", "lat"), None),
            P(("lon", "lat")),
            P(("lon", "lat")),
            P(),
            P(),
            P("lon", "lat"),
            P(None, "lon", "lat"),
        ),
        out_specs=P(None, "lon", "lat"),
        check_vma=False,
    )
```

```python
import functools

import jax
import jax.numpy as jnp
from jax import lax
from jax.experimental import pallas as pl
from jax.experimental.pallas import tpu as pltpu
from jax.sharding import PartitionSpec as P

STEPS = 2
MESH = pl.DeviceIdType.MESH
HIGHEST = lax.Precision.HIGHEST
NT = (((1,), (1,)), ((), ()))
BF16 = jnp.bfloat16
F32 = jnp.float32


def with_halo(x, sides, width, wrap):
    for axis, dim in sides:
        size, length = (lax.axis_size(axis), x.shape[dim])
        up = [(i, (i + 1) % size) for i in range(size if wrap else size - 1)]
        down = [(j, i) for i, j in up]
        last = lax.slice_in_dim(x, length - width, length, axis=dim)
        first = lax.slice_in_dim(x, 0, width, axis=dim)
        before = lax.ppermute(last, axis, up)
        after = lax.ppermute(first, axis, down)
        x = jnp.concatenate([before, x, after], axis=dim)
    return x


def stencil(spread, middle, weights):
    return (
        middle * spread[:, 1:-1, 1:-1]
        + weights[0] * spread[:, :-2, 1:-1]
        + weights[1] * spread[:, 2:, 1:-1]
        + weights[2] * spread[:, 1:-1, :-2]
        + weights[3] * spread[:, 1:-1, 2:]
    )


def plain(obs_values, obs_owner, obs_cell, obs_count, obs_map, column_mix, center, neighbor):
    lon_count = lax.axis_size("lon")
    rows, width = obs_values.shape
    capacity = 2 * rows // lon_count
    slots = lon_count * capacity
    lon_cells, lat_cells = center.shape
    owners = obs_owner[:, 0]
    living = jnp.arange(rows, dtype=jnp.int32) < obs_count[0]
    number = jnp.arange(rows, dtype=jnp.int32)
    same = (owners[:, None] == owners[None, :]) & (number[None, :] < number[:, None])
    earlier = jnp.sum(same.astype(jnp.int32), axis=1)
    target = jnp.where(living, owners * capacity + earlier, -1)
    chosen = jnp.arange(slots, dtype=jnp.int32)[:, None] == target[None, :]
    packed = jnp.dot(chosen.astype(BF16), obs_values, preferred_element_type=F32).astype(BF16)
    places = jnp.sum(jnp.where(chosen, obs_cell[None, :] + 1, 0), axis=1) - 1
    packed = packed.reshape(lon_count, capacity, width)
    places = places.reshape(lon_count, capacity)
    packed = lax.all_to_all(packed, "lon", split_axis=0, concat_axis=0, tiled=True)
    places = lax.all_to_all(places, "lon", split_axis=0, concat_axis=0, tiled=True)
    cells = jnp.arange(lon_cells * lat_cells, dtype=jnp.int32)
    onehot = (places.reshape(slots)[:, None] == cells[None, :]).astype(BF16)
    adjoint = lax.dot_general(
        packed.reshape(slots, width), onehot, (((0,), (0,)), ((), ())), preferred_element_type=F32
    ).reshape(width, lon_cells, lat_cells)
    weight = obs_map.astype(F32)
    for section in range(STEPS):
        weight = jnp.dot(weight, column_mix, precision=HIGHEST)
        spread = with_halo(adjoint, (("lon", 1),), 1, True)
        spread = with_halo(spread, (("lat", 2),), 1, False)
        adjoint = stencil(spread, center, neighbor)
    return jnp.einsum("vb,vij->bij", weight, adjoint, precision=HIGHEST)


def iota(shape, dim):
    return lax.broadcasted_iota(jnp.int32, shape, dim)


def onehot_of(labels, count):
    return jnp.where(iota((count, labels.shape[1]), 0) == labels, 1.0, 0.0).astype(BF16)


def route_kernel(
    lon_n, lat_n,
    values_in, owner_in, cell_in, count, obs_map_in, mix_in, center_in, neighbor_in,
    f_out, halo_out, edge_out, corner_out, wlon_out, wlat_out, weight_out,
    send, recv, fsend, halo, esend, edge, corner, wlon_send, wlon, wlat_send, wlat,
    a_send, a_recv, h_send, h_recv,
    values, owner, cell, obs_map, mix, center, neighbor, in_sem,
):
    pairs_in = [
        (owner_in, owner), (cell_in, cell), (values_in, values), (center_in, center),
        (neighbor_in, neighbor), (obs_map_in, obs_map), (mix_in, mix),
    ]
    fetches = [pltpu.make_async_copy(a, b, in_sem.at[n]) for n, (a, b) in enumerate(pairs_in)]
    for fetch in fetches:
        fetch.start()
    me, band = lax.axis_index("lon"), lax.axis_index("lat")
    east, west = lax.rem(me + 1, lon_n), lax.rem(me + lon_n - 1, lon_n)
    north, south = lax.rem(band + 1, lat_n), lax.rem(band + lat_n - 1, lat_n)
    barrier = pltpu.get_barrier_semaphore()
    partners = [(lax.rem(me + k, lon_n), band) for k in range(1, lon_n)]
    partners += [(a, b) for a in (me, east, west) for b in (north, south)]
    for partner in partners:
        pl.semaphore_signal(barrier, inc=1, device_id=partner, device_id_type=MESH)

    lon_cells, lat_cells = center.shape
    rows, width = values.shape
    cap = 2 * rows // lon_n
    for fetch in fetches[:3]:
        fetch.wait()
    own, place = owner[...], cell[...]
    owned = iota((16, rows), 0) == own
    before = jnp.where(iota((rows, rows), 0) < iota((rows, rows), 1), 1.0, 0.0).astype(BF16)
    prior = jnp.dot(jnp.where(owned, 1.0, 0.0).astype(BF16), before, preferred_element_type=F32)
    position = jnp.sum(jnp.where(owned, prior, 0.0), axis=0, keepdims=True).astype(jnp.int32)
    target = jnp.where(iota((1, rows), 1) < count[0], own * cap + position, -1)
    chosen = onehot_of(target, lon_n * cap)
    i, j = place // lat_cells, place % lat_cells
    side = jnp.where(j < 2, j, jnp.where(j >= lat_cells - 2, j - (lat_cells - 4), 4))
    sub = iota((16, rows), 0)
    labels = jnp.where(
        sub == 0,
        i // 2,
        jnp.where(sub == 1, (i % 2) * lat_cells + j, jnp.where(sub == 2, side * lon_cells + i, 0)),
    ).astype(F32)
    turned = jnp.concatenate([values[...].astype(F32).T, labels], axis=0).astype(BF16)
    packed = lax.dot_general(turned, chosen, NT, preferred_element_type=F32).astype(BF16)
    for o in range(lon_n):
        send[o] = packed[:, o * cap : (o + 1) * cap]

    for fetch in fetches[3:5]:
        fetch.wait()
    weights = [center[...]] + [neighbor[k] for k in range(4)]
    wlon_send[...] = jnp.zeros_like(wlon_send)
    for k in range(5):
        wlon_send[0, k : k + 1, :] = weights[k][0:1]
        wlon_send[1, k : k + 1, :] = weights[k][lon_cells - 1 : lon_cells]
    stacked = jnp.concatenate(weights + [jnp.zeros((128 - 5 * lon_cells, lat_cells), F32)], axis=0).T
    wlat_send[0] = stacked[0:8]
    wlat_send[1] = stacked[lat_cells - 8 : lat_cells]

    pl.semaphore_wait(barrier, len(partners))

    def copy(src, dst, sem_out, sem_in, device):
        return pltpu.make_async_remote_copy(
            src_ref=src, dst_ref=dst, send_sem=sem_out, recv_sem=sem_in,
            device_id=device, device_id_type=MESH,
        )

    moves = []
    for k in range(1, lon_n):
        to = lax.rem(me + k, lon_n)
        moves.append(copy(send.at[to], recv.at[k], a_send.at[k - 1], a_recv.at[k - 1], (to, band)))
        moves[-1].start()
    later = []

    def start_later(src, dst, device):
        n = len(later)
        later.append(copy(src, dst, h_send.at[n], h_recv.at[n], device))
        later[-1].start()

    start_later(wlon_send.at[1], wlon.at[0], (east, band))
    start_later(wlon_send.at[0], wlon.at[1], (west, band))
    start_later(wlat_send.at[1], wlat.at[0], (me, north))
    start_later(wlat_send.at[0], wlat.at[1], (me, south))
    recv[0] = send[me]

    for fetch in fetches[5:]:
        fetch.wait()
    weight = obs_map[...].astype(F32)
    for section in range(STEPS):
        weight = jnp.dot(weight, mix[...], precision=HIGHEST, preferred_element_type=F32)
    weight = weight.T
    high = weight.astype(BF16)
    low = (weight - high.astype(F32)).astype(BF16)
    weight_out[...] = jnp.concatenate([high, high, low], axis=1)

    for move in moves:
        move.wait()

    arrived = jnp.concatenate([recv[k, 0:width, :] for k in range(lon_n)], axis=1)
    marks = jnp.concatenate([recv[k, width : width + 16, :] for k in range(lon_n)], axis=1)
    marks = marks.astype(F32).astype(jnp.int32)
    pair, column, rim = marks[0:1], marks[1:2], marks[2:3]
    columns = onehot_of(column, 2 * lat_cells)

    def masked(p):
        return arrived * jnp.where(pair == p, 1.0, 0.0).astype(BF16)

    def spread(pairs):
        left = jnp.concatenate([masked(p) for p in pairs], axis=0)
        out = lax.dot_general(left, columns, NT, preferred_element_type=F32).astype(BF16)
        for n, p in enumerate(pairs):
            for half in range(2):
                yield 2 * p + half, out[n * width : (n + 1) * width, half * lat_cells : (half + 1) * lat_cells]

    pairs = lon_cells // 2
    for n, (at, block) in enumerate(spread((0, pairs - 1))):
        fsend[n] = block
        f_out[at] = block
    start_later(fsend.at[pl.ds(2, 2)], halo.at[pl.ds(0, 2)], (east, band))
    start_later(fsend.at[pl.ds(0, 2)], halo.at[pl.ds(2, 2)], (west, band))
    rims = onehot_of(rim, 4 * lon_cells)
    esend[...] = lax.dot_general(rims, arrived, NT, preferred_element_type=F32).astype(BF16)
    start_later(esend.at[pl.ds(32, 32)], edge.at[pl.ds(0, 32)], (me, north))
    start_later(esend.at[pl.ds(0, 32)], edge.at[pl.ds(32, 32)], (me, south))
    start_later(esend.at[pl.ds(48, 16)], corner.at[0], (east, north))
    start_later(esend.at[pl.ds(0, 16)], corner.at[1], (east, south))
    start_later(esend.at[pl.ds(48, 16)], corner.at[2], (west, north))
    start_later(esend.at[pl.ds(0, 16)], corner.at[3], (west, south))
    for at, block in spread(range(1, pairs - 1)):
        f_out[at] = block
    for move in later:
        move.wait()
    halo_out[...] = halo[...]
    edge_out[0:64] = edge[...]
    edge_out[64:80] = esend[0:16]
    edge_out[80:96] = esend[48:64]
    corner_out[...] = corner[...]
    wlon_out[...] = wlon[...]
    wlat_out[...] = wlat[...]


def apply_kernel(
    lat_n, f, halo, edge, corner, wlon, wlat, weight, center, neighbor, out, first, grid_values
):
    lon_cells, lat_cells = center.shape
    width = f.shape[1]

    @pl.when(pl.program_id(0) == 0)
    def _():
        band = lax.axis_index("lat")
        keeps = [jnp.where(band > 0, 1.0, 0.0), jnp.where(band < lat_n - 1, 1.0, 0.0)]
        rim = edge[...].astype(F32)
        south2, south1, north1, north2, inner_s, inner_n = (rim[16 * n : 16 * (n + 1)] for n in range(6))
        corners = corner[...].astype(F32)
        cws, cwn, ces, cen = corners[0, 15:16], corners[1, 15:16], corners[2, 0:1], corners[3, 0:1]

        def rim_step(turned, here, west, east, below, above):
            w = [turned[16 * k : 16 * (k + 1)] for k in range(5)]
            up = jnp.concatenate([west, here[:-1]], axis=0)
            down = jnp.concatenate([here[1:], east], axis=0)
            return w[0] * here + w[1] * up + w[2] * down + w[3] * below + w[4] * above

        tall = jnp.zeros((120, 128), F32)
        ws = jnp.concatenate([wlat[0], tall], axis=0).T[:, 7:8]
        wn = jnp.concatenate([wlat[1], tall], axis=0).T[:, 0:1]
        step_s = rim_step(ws, south1, cws, ces, south2, inner_s)
        step_n = rim_step(wn, north1, cwn, cen, inner_n, north2)
        table = jnp.concatenate(
            [south1 * keeps[0], north1 * keeps[1], step_s * keeps[0], step_n * keeps[1],
             cws * keeps[0], cwn * keeps[1], ces * keeps[0], cen * keeps[1],
             jnp.zeros((60, width), F32)], axis=0,
        ).T
        lane = iota((width, lat_cells), 1)

        def value(n):
            if n < 0:
                return halo[n + 2].astype(F32)
            return halo[n - lon_cells + 2].astype(F32) if n >= lon_cells else f[n].astype(F32)

        def weights_at(n):
            if n < 0:
                return [wlon[0, k : k + 1, :] for k in range(5)]
            if n >= lon_cells:
                return [wlon[1, k : k + 1, :] for k in range(5)]
            return [center[n : n + 1, :]] + [neighbor[k, n : n + 1, :] for k in range(4)]

        def step(n, here, west, east, s, t):
            w = weights_at(n)
            below = jnp.where(lane == 0, table[:, s : s + 1], pltpu.roll(here, 1, 1))
            above = jnp.where(lane == lat_cells - 1, table[:, t : t + 1], pltpu.roll(here, lat_cells - 1, 1))
            return w[0] * here + w[1] * west + w[2] * east + w[3] * below + w[4] * above

        for n in range(-1, lon_cells + 1):
            s, t = (64, 65) if n < 0 else (66, 67) if n >= lon_cells else (n, 16 + n)
            first[n + 1] = step(n, value(n), value(n - 1), value(n + 1), s, t)
        for n in range(lon_cells):
            done = step(n, first[n + 1], first[n], first[n + 2], 32 + n, 48 + n)
            high = done.astype(BF16)
            at = slice(n * lat_cells, (n + 1) * lat_cells)
            grid_values[0:width, at] = high
            grid_values[width : 2 * width, at] = (done - high.astype(F32)).astype(BF16)
            grid_values[2 * width : 3 * width, at] = high

    result = jnp.dot(weight[...], grid_values[...], preferred_element_type=F32)
    chunk = weight.shape[0]
    for n in range(lon_cells):
        out[pl.ds(n, chunk, stride=lon_cells), :] = result[:, n * lat_cells : (n + 1) * lat_cells]


def fast(obs_values, obs_owner, obs_cell, obs_count, obs_map, column_mix, center, neighbor):
    lon_n, lat_n = lax.axis_size("lon"), lax.axis_size("lat")
    rows, width = obs_values.shape
    extent = column_mix.shape[0]
    lon_cells, lat_cells = center.shape
    cap = 2 * rows // lon_n
    vmem, shape = pl.BlockSpec(memory_space=pltpu.VMEM), jax.ShapeDtypeStruct
    hbm = pl.BlockSpec(memory_space=pltpu.HBM)
    parts = pl.pallas_call(
        functools.partial(route_kernel, lon_n, lat_n),
        out_shape=[
            shape((lon_cells, width, lat_cells), BF16),
            shape((4, width, lat_cells), BF16),
            shape((96, width), BF16),
            shape((4, 16, width), BF16),
            shape((2, 8, lat_cells), F32),
            shape((2, 8, 128), F32),
            shape((extent, 3 * width), BF16),
        ],
        in_specs=[hbm] * 3 + [pl.BlockSpec(memory_space=pltpu.SMEM)] + [hbm] * 4,
        out_specs=[vmem] * 7,
        scratch_shapes=[
            pltpu.VMEM((lon_n, width + 16, cap), BF16),
            pltpu.VMEM((lon_n, width + 16, cap), BF16),
            pltpu.VMEM((4, width, lat_cells), BF16),
            pltpu.VMEM((4, width, lat_cells), BF16),
            pltpu.VMEM((64, width), BF16),
            pltpu.VMEM((64, width), BF16),
            pltpu.VMEM((4, 16, width), BF16),
            pltpu.VMEM((2, 8, lat_cells), F32),
            pltpu.VMEM((2, 8, lat_cells), F32),
            pltpu.VMEM((2, 8, 128), F32),
            pltpu.VMEM((2, 8, 128), F32),
            pltpu.SemaphoreType.DMA((lon_n - 1,)),
            pltpu.SemaphoreType.DMA((lon_n - 1,)),
            pltpu.SemaphoreType.DMA((12,)),
            pltpu.SemaphoreType.DMA((12,)),
            pltpu.VMEM(obs_values.shape, BF16),
            pltpu.VMEM((1, rows), jnp.int32),
            pltpu.VMEM((1, rows), jnp.int32),
            pltpu.VMEM(obs_map.shape, BF16),
            pltpu.VMEM(column_mix.shape, F32),
            pltpu.VMEM(center.shape, F32),
            pltpu.VMEM(neighbor.shape, F32),
            pltpu.SemaphoreType.DMA((7,)),
        ],
        compiler_params=pltpu.CompilerParams(
            collective_id=0, has_side_effects=True, vmem_limit_bytes=62 * 2**20
        ),
    )(obs_values, obs_owner.reshape(1, rows), obs_cell.reshape(1, rows), obs_count, obs_map, column_mix, center, neighbor)
    chunk = extent // 2
    whole = [pl.BlockSpec(x.shape, functools.partial(lambda d, n: (0,) * d, x.ndim)) for x in parts[:6]]
    out = pl.pallas_call(
        functools.partial(apply_kernel, lat_n),
        grid=(extent // chunk,),
        out_shape=shape((extent * lon_cells, lat_cells), F32),
        in_specs=whole + [
            pl.BlockSpec((chunk, 3 * width), lambda n: (n, 0)),
            pl.BlockSpec(center.shape, lambda n: (0, 0)),
            pl.BlockSpec(neighbor.shape, lambda n: (0, 0, 0)),
        ],
        out_specs=pl.BlockSpec((chunk * lon_cells, lat_cells), lambda n: (n, 0)),
        scratch_shapes=[
            pltpu.VMEM((lon_cells + 2, width, lat_cells), F32),
            pltpu.VMEM((3 * width, lon_cells * lat_cells), BF16),
        ],
        compiler_params=pltpu.CompilerParams(vmem_limit_bytes=62 * 2**20),
    )(*parts, center, neighbor)
    return out.reshape(extent, lon_cells, lat_cells)


def on_device(*arrays):
    rows, width = arrays[0].shape
    lon_n = lax.axis_size("lon")
    fits = 2 * rows // lon_n == 128 and width == 128 and arrays[6].shape == (16, 128) and lon_n <= 16
    return (fast if fits else plain)(*arrays)


def solution(mesh):
    return jax.shard_map(
        on_device,
        mesh=mesh,
        in_specs=(
            P(("lon", "lat"), None),
            P(("lon", "lat"), None),
            P(("lon", "lat")),
            P(("lon", "lat")),
            P(),
            P(),
            P("lon", "lat"),
            P(None, "lon", "lat"),
        ),
        out_specs=P(None, "lon", "lat"),
        check_vma=False,
    )
```
